32 devices in a mesh: groups: 2 (over y), ctx: 4 (over z), dp: 2 (over x), head: 2 (over core).
Axes of the slice: x: 2, y: 2, z: 4, core: 2. Of those that a mesh axis runs over, the one named last changes fastest.
Arguments:
- queries: bfloat16 [4, 2048, 32, 128], P(('groups', 'dp'), 'ctx', 'head'), parts along dimension 0, may hold values from -128 to 128
- key_states: bfloat16 [4, 2048, 4, 128], P(('groups', 'dp'), 'ctx', 'head'), parts along dimension 0, may hold values from -7 to 7
- value_states: bfloat16 [4, 2048, 4, 128], P(('groups', 'dp'), 'ctx', 'head'), parts along dimension 0, may hold values from -6 to 6
- teacher_out: bfloat16 [4, 2048, 32, 128], P(('groups', 'dp'), 'ctx', 'head'), parts along dimension 0, may hold values from -6 to 6
- selection: int32 [4, 32, 4, 16], P(('groups', 'dp'), 'ctx', 'head'), parts along dimension 0, may hold values from -1 to 31, as said below
- compress_keys: float32 [4, 64, 128], P('head'), may hold values from -0.75 to 0.75
- compress_values: float32 [4, 64, 128], P('head'), may hold values from -0.75 to 0.75
- gate_weights: float32 [32, 2, 128], P('head'), may hold values from -0.5 to 0.5
Outputs:
- key_grad: bfloat16 [4, 2048, 4, 128], P(('groups', 'dp'), 'ctx', 'head'), parts along dimension 0
- value_grad: bfloat16 [4, 2048, 4, 128], P(('groups', 'dp'), 'ctx', 'head'), parts along dimension 0
- compress_key_grad: float32 [8, 64, 128], P(('groups', 'head')), parts along dimension 0
- compress_value_grad: float32 [8, 64, 128], P(('groups', 'head')), parts along dimension 0
- gate_grad: float32 [64, 2, 128], P(('groups', 'head')), parts along dimension 0
The draws below stay inside these ranges and needn't reach their ends.
There are 2 independent parts, one for each index of `groups`. The reference program is written for one: setup_inputs(seed, part) draws one part's arguments, and reference() takes and returns one part's arrays. A program takes and returns all parts, laid end to end along the dimension named above; an argument that names none is the same for every part. Nothing has to cross between parts.
Inputs may be any that keep to these rules, and one draw needn't show every extreme that they name: `selection`: each list of query block j and key-value head names distinct blocks up to j, always j and 0; unused slots hold -1 and come last. Of the blocks named by the query blocks of one index of ctx, for one context and key-value head, those held by another index number at most 4 for each other index; on the last index of ctx exactly 4 for every other index.
All inputs are finite; a program needn't handle non-finite values.
Results may differ from the reference program's by a relative error of at most 0.003.
The reference program's roundings to bfloat16 on the way (of `comp_keys`, `comp_values`, `sel_rounded`, `sel_back` and `score_grad`) count: a program that leaves them out, or rounds other values in their place, can miss the bound.
Values may be sent and summed in bfloat16 or wider, within the bound.
A program may use at most 128 MiB of HBM per device.

```python
import math
import jax
import jax.numpy as jnp
from jax import lax

HEADS = 32
KVH = 4
HD = 128
BLOCK = 64
SEL = 16
GROUP = 8
LENGTH = 2048
NB = 32
BPD = 8
CAP = 4
CTXS = 2


def key_field(key):
    field = jnp.clip(jax.random.normal(key, (CTXS, LENGTH, KVH, HD), jnp.float32), -6.0, 6.0)
    return field


def draw_key_states(key, part):
    shared = key_field(key)
    return shared.astype(jnp.bfloat16)


def draw_queries(key, part):
    key = jax.random.fold_in(key, 11)
    field = jnp.clip(jax.random.normal(key, (CTXS, LENGTH, HEADS, HD), jnp.float32), -6.0, 6.0)
    return field.astype(jnp.bfloat16)


def draw_selection(key, part):
    key = jax.random.fold_in(key, 5)
    first_key, second_key = jax.random.split(key)
    ctx_count = NB // BPD
    blocks = jnp.arange(NB)
    holder = blocks // BPD
    within = blocks % BPD
    priority = jax.random.randint(first_key, (CTXS, ctx_count, KVH, NB), 0, 1 << 20) * BPD + within
    priority = priority + (blocks == 0).astype(jnp.int32) * (1 << 28)
    same_holder = holder[:, None] == holder[None, :]
    higher = priority[..., :, None] > priority[..., None, :]
    rank = jnp.sum((higher & same_holder).astype(jnp.int32), axis=-2)
    devices = jnp.arange(ctx_count)
    member = (rank < CAP) & (holder[None, :] < devices[:, None])[None, :, None, :]
    label = holder * CAP + rank
    member_rows = jnp.repeat(member, BPD, axis=1)
    label_rows = jnp.repeat(label, BPD, axis=1)
    queried = jnp.arange(NB)
    query_device = (queried // BPD)[None, :, None, None]
    query_within = (queried % BPD)[None, :, None, None]
    current = queried[None, :, None, None]
    target = blocks[None, None, None, :]
    forced = (target == 0) | (target == current) | member_rows & (label_rows % BPD == query_within)
    eligible = (target == current) | (target < current) & ((holder[None, None, None, :] == query_device) | member_rows)
    random_part = jax.random.randint(second_key, member_rows.shape, 0, 1 << 12)
    scores = jnp.where(forced, (1 << 24) + target, jnp.where(eligible, random_part * NB + target, -1 - target))
    scores = scores.astype(jnp.int32)
    top_scores, chosen = lax.top_k(scores, SEL)
    return jnp.where(top_scores >= 0, chosen, -1).astype(jnp.int32)


def levels(key, extent, shards, low, high):
    gain, own = 1.0, jax.random.fold_in(key, 6)
    for dim, shards_of in shards:
        heights = jnp.exp(jax.random.uniform(jax.random.fold_in(own, dim), (shards_of,), jnp.float32, low / len(shards), high / len(shards)))
        gain = gain * jnp.repeat(heights, extent[dim] // shards_of).reshape([-1 if axis == dim else 1 for axis in range(len(extent))])
    return gain


def normal_values(own_key, dims, spread, bound, cuts=(), held_as=jnp.bfloat16):
    array = spread * jax.random.normal(own_key, dims, jnp.float32)
    if cuts:
        array = array * levels(own_key, dims, cuts, -0.22, 0.18)
    return jnp.clip(array, -bound, bound).astype(held_as)


def setup_inputs(seed: int = 0, part: int = 0) -> dict:
    keys = jax.random.split(jax.random.key(seed), 9)
    part_keys = jax.random.split(jax.random.fold_in(keys[8], part), 9)
    queries = draw_queries(jax.random.fold_in(jax.random.fold_in(keys[8], part), 71), part)
    key_states = draw_key_states(jax.random.fold_in(jax.random.fold_in(keys[8], part), 71), part)
    value_states = normal_values(part_keys[2], (CTXS, LENGTH, KVH, HD), 1.0, 6.0, ((0, 2), (1, 4), (2, 2)))
    teacher_out = normal_values(part_keys[3], (CTXS, LENGTH, HEADS, HD), 1.0, 6.0, ((0, 2), (1, 4), (2, 2)))
    selection = draw_selection(jax.random.fold_in(jax.random.fold_in(keys[8], part), 71), part)
    compress_keys = normal_values(keys[5], (KVH, BLOCK, HD), BLOCK ** -0.5, 0.75, ((0, 2),), jnp.float32)
    compress_values = normal_values(keys[6], (KVH, BLOCK, HD), BLOCK ** -0.5, 0.75, ((0, 2),), jnp.float32)
    gate_weights = normal_values(keys[7], (HEADS, 2, HD), HD ** -0.5, 0.5, ((0, 2),), jnp.float32)
    return {"queries": queries, "key_states": key_states, "value_states": value_states, "teacher_out": teacher_out, "selection": selection, "compress_keys": compress_keys, "compress_values": compress_values, "gate_weights": gate_weights}


HIGHEST = lax.Precision.HIGHEST
MASKED = -1e+30

def masked_softmax(scores, usable):
    peaks = lax.optimization_barrier(jnp.max(jnp.where(usable, scores, MASKED), axis=-1, keepdims=True))
    raised = jnp.where(usable, jnp.exp(jnp.where(usable, scores, peaks) - peaks), 0.0)
    return raised / lax.optimization_barrier(jnp.sum(raised, axis=-1, keepdims=True))

def branch_grads(weights, rounded, back_wide, query_wide, piece_values, factor):
    weight_grad = jnp.einsum('tgnd,gkd->gtnk', back_wide, piece_values.astype(jnp.float32))
    row_total = lax.optimization_barrier(jnp.sum(weights * weight_grad, axis=-1, keepdims=True))
    score_grad = (factor * weights * (weight_grad - row_total)).astype(jnp.bfloat16)
    value_part = jnp.einsum('gtnk,tgnd->gkd', rounded.astype(jnp.float32), back_wide)
    key_part = jnp.einsum('gtnk,tgnd->gkd', score_grad.astype(jnp.float32), query_wide)
    return (key_part, value_part)

def attend_block(queried, teacher_rows, piece_keys, piece_values, key_usable, comp_keys, comp_values, comp_usable, gate_grouped):
    factor = queried.shape[-1] ** (-0.5)
    query_wide = queried.astype(jnp.float32)
    sel_scores = jnp.einsum('tgnd,gkd->gtnk', query_wide, piece_keys.astype(jnp.float32)) * factor
    sel_weights = masked_softmax(sel_scores, key_usable[:, :, None, :])
    sel_rounded = sel_weights.astype(jnp.bfloat16)
    sel_out = jnp.einsum('gtnk,gkd->tgnd', sel_rounded.astype(jnp.float32), piece_values.astype(jnp.float32))
    comp_scores = jnp.einsum('tgnd,gkd->gtnk', query_wide, comp_keys.astype(jnp.float32)) * factor
    comp_weights = masked_softmax(comp_scores, comp_usable[None, None, None, :])
    comp_rounded = comp_weights.astype(jnp.bfloat16)
    comp_out = jnp.einsum('gtnk,gkd->tgnd', comp_rounded.astype(jnp.float32), comp_values.astype(jnp.float32))
    gate_logits = jnp.einsum('tgnd,gnrd->tgnr', query_wide, gate_grouped, precision=HIGHEST)
    gates = jax.nn.sigmoid(gate_logits)
    mixed = gates[..., 0:1] * comp_out + gates[..., 1:2] * sel_out
    error = mixed - teacher_rows.astype(jnp.float32)
    gate_terms = jnp.stack([lax.optimization_barrier(jnp.sum(error * comp_out, axis=-1)), lax.optimization_barrier(jnp.sum(error * sel_out, axis=-1))], axis=-1) * (gates * (1.0 - gates))
    gate_part = jnp.einsum('tgnr,tgnd->gnrd', gate_terms, query_wide, precision=HIGHEST)
    sel_back = (gates[..., 1:2] * error).astype(jnp.bfloat16).astype(jnp.float32)
    comp_back = (gates[..., 0:1] * error).astype(jnp.bfloat16).astype(jnp.float32)
    sel_key, sel_value = branch_grads(sel_weights, sel_rounded, sel_back, query_wide, piece_values, factor)
    comp_key, comp_value = branch_grads(comp_weights, comp_rounded, comp_back, query_wide, comp_values, factor)
    return (sel_key, sel_value, comp_key, comp_value, gate_part)

def context_grads(queries, key_states, value_states, teacher_out, selection, compress_keys, compress_values, gate_weights):
    key_blocks = key_states.reshape(NB, BLOCK, KVH, HD)
    value_blocks = value_states.reshape(NB, BLOCK, KVH, HD)
    comp_keys = jnp.einsum('bugd,gud->gbd', key_blocks.astype(jnp.float32), compress_keys, precision=HIGHEST).astype(jnp.bfloat16)
    comp_values = jnp.einsum('bugd,gud->gbd', value_blocks.astype(jnp.float32), compress_values, precision=HIGHEST).astype(jnp.bfloat16)
    key_pieces = key_blocks.transpose(2, 0, 1, 3)
    value_pieces = value_blocks.transpose(2, 0, 1, 3)
    query_blocks = queries.reshape(NB, BLOCK, KVH, GROUP, HD)
    teacher_blocks = teacher_out.reshape(NB, BLOCK, KVH, GROUP, HD)
    head_range = jnp.arange(KVH)[:, None]
    offsets = jnp.arange(BLOCK)
    causal = offsets[None, :] <= offsets[:, None]
    gate_grouped = gate_weights.reshape(KVH, GROUP, 2, HD)
    block_range = jnp.arange(NB).astype(jnp.int32)

    def advance(carry, items):
        key_acc, value_acc, comp_key_acc, comp_value_acc, gate_acc = carry
        queried, teacher_rows, chosen, current = items
        usable = chosen >= 0
        lookup = jnp.where(usable, chosen, 0).astype(jnp.int32)
        piece_keys = key_pieces[head_range, lookup].reshape(KVH, SEL * BLOCK, HD)
        piece_values = value_pieces[head_range, lookup].reshape(KVH, SEL * BLOCK, HD)
        own_block = chosen == current
        key_usable = usable[:, None, :, None] & (jnp.logical_not(own_block)[:, None, :, None] | causal[None, :, None, :])
        key_usable = key_usable.reshape(KVH, BLOCK, SEL * BLOCK)
        comp_usable = block_range <= current
        sel_key, sel_value, comp_key, comp_value, gate_part = attend_block(queried, teacher_rows, piece_keys, piece_values, key_usable, comp_keys, comp_values, comp_usable, gate_grouped)
        key_acc = key_acc.at[head_range, lookup].add(sel_key.reshape(KVH, SEL, BLOCK, HD))
        value_acc = value_acc.at[head_range, lookup].add(sel_value.reshape(KVH, SEL, BLOCK, HD))
        return ((key_acc, value_acc, comp_key_acc + comp_key, comp_value_acc + comp_value, gate_acc + gate_part), None)
    start = (jnp.zeros((KVH, NB, BLOCK, HD), jnp.float32), jnp.zeros((KVH, NB, BLOCK, HD), jnp.float32), jnp.zeros((KVH, NB, HD), jnp.float32), jnp.zeros((KVH, NB, HD), jnp.float32), jnp.zeros((KVH, GROUP, 2, HD), jnp.float32))
    finish, unused = lax.scan(advance, start, (query_blocks, teacher_blocks, selection, block_range))
    key_acc, value_acc, comp_key_acc, comp_value_acc, gate_acc = finish
    key_total = key_acc + compress_keys[:, None, :, :] * comp_key_acc[:, :, None, :]
    value_total = value_acc + compress_values[:, None, :, :] * comp_value_acc[:, :, None, :]
    key_grad = key_total.transpose(1, 2, 0, 3).reshape(LENGTH, KVH, HD).astype(jnp.bfloat16)
    value_grad = value_total.transpose(1, 2, 0, 3).reshape(LENGTH, KVH, HD).astype(jnp.bfloat16)
    weight_key = jnp.einsum('gbd,bugd->gud', comp_key_acc, key_blocks.astype(jnp.float32), precision=HIGHEST)
    weight_value = jnp.einsum('gbd,bugd->gud', comp_value_acc, value_blocks.astype(jnp.float32), precision=HIGHEST)
    return (key_grad, value_grad, weight_key, weight_value, gate_acc.reshape(HEADS, 2, HD))

def reference(queries, key_states, value_states, teacher_out, selection, compress_keys, compress_values, gate_weights):

    def one_context(items):
        return context_grads(items[0], items[1], items[2], items[3], items[4], compress_keys, compress_values, gate_weights)
    key_grad, value_grad, weight_key, weight_value, gate_sum = lax.map(one_context, (queries, key_states, value_states, teacher_out, selection))
    divisor = math.sqrt(CTXS * LENGTH)
    return (key_grad, value_grad, lax.optimization_barrier(jnp.sum(weight_key, axis=0)) / divisor, lax.optimization_barrier(jnp.sum(weight_value, axis=0)) / divisor, lax.optimization_barrier(jnp.sum(gate_sum, axis=0)) / divisor)
```

```python
import functools
import math

import jax
import jax.numpy as jnp
from jax import lax
from jax.experimental import pallas as pl
from jax.experimental.pallas import tpu as pltpu
from jax.sharding import PartitionSpec as P

HIGHEST = lax.Precision.HIGHEST
MASKED = -1e30
NT = (((1,), (1,)), ((), ()))
NN = (((1,), (0,)), ((), ()))
TN = (((0,), (0,)), ((), ()))


def dot(a, b, dims):
    return lax.dot_general(a, b, dims, preferred_element_type=jnp.float32)


def fold(x, op):
    return op(x.reshape(x.shape[0] // 8, 8, x.shape[1]), axis=0)


def attend_kernel(
    dims,
    bias_ref,
    q_ref,
    t_ref,
    k_ref,
    v_ref,
    ck_ref,
    cv_ref,
    gw_ref,
    cur_ref,
    dk_ref,
    dv_ref,
    dck_ref,
    dcv_ref,
    dgw_ref,
    s_scr,
    d_scr,
    vt_scr,
    ot_scr,
    tri_scr,
):
    kv_heads, group, span, remote_slots, own_blocks, chunk_slots, pair = dims
    slots = remote_slots + own_blocks
    chunk = chunk_slots * span
    head_dim = q_ref.shape[-1]
    rows = span * group
    factor = head_dim ** (-0.5)
    power = factor * math.log2(math.e)
    j = pl.program_id(0)
    chunks = (remote_slots + j) // chunk_slots + 1

    @pl.when(j == 0)
    def _():
        dk_ref[...] = jnp.zeros_like(dk_ref)
        dv_ref[...] = jnp.zeros_like(dv_ref)
        dck_ref[...] = jnp.zeros_like(dck_ref)
        dcv_ref[...] = jnp.zeros_like(dcv_ref)
        dgw_ref[...] = jnp.zeros_like(dgw_ref)
        key_at = lax.broadcasted_iota(jnp.int32, (span, rows), 0)
        row_at = lax.broadcasted_iota(jnp.int32, (span, rows), 1) // group
        tri_scr[...] = jnp.where(key_at <= row_at, 0.0, MASKED)

        def turn(c, _):
            at = pl.ds(pl.multiple_of(c * chunk, chunk), chunk)
            for g in range(kv_heads):
                vt_scr[g, :, at] = v_ref[g, at, :].astype(jnp.float32).T.astype(jnp.bfloat16)
            return 0

        lax.fori_loop(0, slots // chunk_slots, turn, 0)

    for base in range(0, kv_heads, pair):
        heads = [(p, base + p) for p in range(pair)]
        wide = {}
        narrow = {}
        for p, g in heads:
            wide[p] = (
                q_ref[...].astype(jnp.float32)[:, g * group : (g + 1) * group, :]
            )
            narrow[p] = wide[p].reshape(rows, head_dim).astype(jnp.bfloat16)

        def scores(c, peaks):
            at = pl.ds(pl.multiple_of(c * chunk, chunk), chunk)
            out = []
            for p, g in heads:
                s = dot(k_ref[g, at, :], narrow[p], NT)
                parts = []
                for i in range(chunk_slots):
                    b = bias_ref[(j * kv_heads + g) * slots + c * chunk_slots + i]
                    parts.append(s[i * span : (i + 1) * span] + b)
                s = jnp.concatenate(parts, axis=0)
                s_scr[p, at, :] = s
                out.append(jnp.maximum(peaks[p], fold(s, jnp.max)))
            return tuple(out)

        peaks = lax.fori_loop(
            0, chunks, scores, tuple(jnp.full((8, rows), MASKED, jnp.float32) for _ in heads)
        )
        own = pl.ds(pl.multiple_of((remote_slots + j) * span, span), span)
        peak = {}
        for p, g in heads:
            s = dot(k_ref[g, own, :], narrow[p], NT) + tri_scr[...]
            s_scr[p, own, :] = s
            peak[p] = jnp.max(
                jnp.maximum(peaks[p], fold(s, jnp.max)), axis=0, keepdims=True
            )

        def raise_all(c, sums):
            at = pl.ds(pl.multiple_of(c * chunk, chunk), chunk)
            out = []
            for p, g in heads:
                e = jnp.exp2((s_scr[p, at, :] - peak[p]) * power)
                s_scr[p, at, :] = e
                out.append(sums[p] + fold(e, jnp.sum))
            return tuple(out)

        sums = lax.fori_loop(
            0, chunks, raise_all, tuple(jnp.zeros((8, rows), jnp.float32) for _ in heads)
        )
        inverse = {p: 1.0 / jnp.sum(sums[p], axis=0, keepdims=True) for p, g in heads}
        ot_scr[...] = jnp.zeros_like(ot_scr)

        def outputs(c, _):
            at = pl.ds(pl.multiple_of(c * chunk, chunk), chunk)
            for p, g in heads:
                w = s_scr[p, at, :] * inverse[p]
                s_scr[p, at, :] = w
                ot_scr[p] += dot(vt_scr[g, :, at], w.astype(jnp.bfloat16), NN)
            return 0

        lax.fori_loop(0, chunks, outputs, 0)

        backs = {}
        for p, g in heads:
            sel_out = ot_scr[p].T
            ck = ck_ref[g]
            cv = cv_ref[g]
            cs = dot(ck, narrow[p], NT)
            at_block = lax.broadcasted_iota(jnp.int32, cs.shape, 0)
            usable = at_block <= cur_ref[0] + j
            cs = jnp.where(usable, cs, MASKED)
            ce = jnp.exp2((cs - jnp.max(cs, axis=0, keepdims=True)) * power)
            cw = ce * (1.0 / jnp.sum(ce, axis=0, keepdims=True))
            cr = cw.astype(jnp.bfloat16)
            comp_out = dot(cv, cr, TN).T
            q3 = wide[p]
            gates = []
            for r in range(2):
                logit = jnp.sum(q3 * gw_ref[g, r][None], axis=-1, keepdims=True)
                gates.append(jax.nn.sigmoid(logit))
            comp3 = comp_out.reshape(span, group, head_dim)
            sel3 = sel_out.reshape(span, group, head_dim)
            t3 = t_ref[...].astype(jnp.float32)[:, g * group : (g + 1) * group, :]
            error = gates[0] * comp3 + gates[1] * sel3 - t3
            for r, branch in ((0, comp3), (1, sel3)):
                term = jnp.sum(error * branch, axis=-1, keepdims=True) * (
                    gates[r] * (1.0 - gates[r])
                )
                dgw_ref[g, r] += jnp.sum(term * q3, axis=0)
            backs[p] = (gates[1] * error).reshape(rows, head_dim).astype(jnp.bfloat16)
            cb = (gates[0] * error).reshape(rows, head_dim).astype(jnp.bfloat16)
            cd = dot(cv, cb, NT)
            total = jnp.sum(cw * cd, axis=0, keepdims=True)
            cg = (factor * cw * (cd - total)).astype(jnp.bfloat16)
            dck_ref[g] += dot(cg, narrow[p], NN)
            dcv_ref[g] += dot(cr, cb, NN)

        def weight_grads(c, totals):
            at = pl.ds(pl.multiple_of(c * chunk, chunk), chunk)
            out = []
            for p, g in heads:
                d = dot(v_ref[g, at, :], backs[p], NT)
                d_scr[p, at, :] = d
                out.append(totals[p] + fold(s_scr[p, at, :] * d, jnp.sum))
            return tuple(out)

        totals = lax.fori_loop(
            0, chunks, weight_grads, tuple(jnp.zeros((8, rows), jnp.float32) for _ in heads)
        )
        total = {p: jnp.sum(totals[p], axis=0, keepdims=True) for p, g in heads}

        def key_grads(c, _):
            at = pl.ds(pl.multiple_of(c * chunk, chunk), chunk)
            for p, g in heads:
                w = s_scr[p, at, :]
                sg = (w * ((d_scr[p, at, :] - total[p]) * factor)).astype(jnp.bfloat16)
                dk_ref[g, at, :] += dot(sg, narrow[p], NN)
                dv_ref[g, at, :] += dot(w.astype(jnp.bfloat16), backs[p], NN)
            return 0

        lax.fori_loop(0, chunks, key_grads, 0)


def attend(queries, teacher, keys, values, comp_keys, comp_values, gate_pairs, bias, first, dims):
    kv_heads, group, span, remote_slots, own_blocks, chunk_slots, pair = dims
    slots = remote_slots + own_blocks
    head_dim = keys.shape[-1]
    all_blocks = comp_keys.shape[1]
    rows = span * group
    whole = pl.BlockSpec(memory_space=pltpu.VMEM)
    scalars = pl.BlockSpec(memory_space=pltpu.SMEM)
    tokens = pl.BlockSpec((span, kv_heads * group, head_dim), lambda j: (j, 0, 0))
    f32 = jnp.float32
    flops = own_blocks * kv_heads * rows * slots * span * head_dim * 10
    return pl.pallas_call(
        functools.partial(attend_kernel, dims),
        grid=(own_blocks,),
        in_specs=[scalars, tokens, tokens, whole, whole, whole, whole, whole, scalars],
        out_specs=[whole] * 5,
        out_shape=[
            jax.ShapeDtypeStruct((kv_heads, slots * span, head_dim), f32),
            jax.ShapeDtypeStruct((kv_heads, slots * span, head_dim), f32),
            jax.ShapeDtypeStruct((kv_heads, all_blocks, head_dim), f32),
            jax.ShapeDtypeStruct((kv_heads, all_blocks, head_dim), f32),
            jax.ShapeDtypeStruct((kv_heads, 2, group, head_dim), f32),
        ],
        scratch_shapes=[
            pltpu.VMEM((pair, slots * span, rows), f32),
            pltpu.VMEM((pair, slots * span, rows), f32),
            pltpu.VMEM((kv_heads, head_dim, slots * span), jnp.bfloat16),
            pltpu.VMEM((pair, head_dim, rows), f32),
            pltpu.VMEM((span, rows), f32),
        ],
        compiler_params=pltpu.CompilerParams(vmem_limit_bytes=60 * 1024 * 1024),
        cost_estimate=pl.CostEstimate(flops=flops, bytes_accessed=8 << 20, transcendentals=0),
    )(bias, queries, teacher, keys, values, comp_keys, comp_values, gate_pairs, first)


def on_device(
    queries,
    key_states,
    value_states,
    teacher_out,
    selection,
    compress_keys,
    compress_values,
    gate_weights,
):
    ctx_count = lax.axis_size("ctx")
    my_index = lax.axis_index("ctx")
    tokens_dev = key_states.shape[1]
    kv_heads = key_states.shape[2]
    head_dim = key_states.shape[3]
    span = compress_keys.shape[1]
    own_blocks = tokens_dev // span
    all_blocks = own_blocks * ctx_count
    group = queries.shape[2] // kv_heads
    key_blocks = key_states[0].reshape(own_blocks, span, kv_heads, head_dim)
    value_blocks = value_states[0].reshape(own_blocks, span, kv_heads, head_dim)
    comp_local = jnp.stack(
        [
            jnp.sum(key_blocks.astype(jnp.float32) * compress_keys.transpose(1, 0, 2)[None], axis=1),
            jnp.sum(
                value_blocks.astype(jnp.float32) * compress_values.transpose(1, 0, 2)[None], axis=1
            ),
        ]
    ).astype(jnp.bfloat16)
    comp_all = lax.all_gather(comp_local, "ctx", axis=1, tiled=True).transpose(0, 2, 1, 3)
    comp_keys, comp_values = comp_all[0], comp_all[1]
    chosen = selection[0]
    pieces = jnp.stack(
        [key_blocks.transpose(2, 0, 1, 3), value_blocks.transpose(2, 0, 1, 3)], axis=2
    )
    capacity = own_blocks // 2
    hits = jnp.any(chosen[..., None] == jnp.arange(all_blocks), axis=2)
    hits = hits.astype(jnp.int32).reshape(own_blocks, kv_heads, ctx_count, own_blocks)
    present = jnp.max(hits, axis=0)
    earlier = jnp.arange(own_blocks)[:, None] < jnp.arange(own_blocks)[None, :]
    slot_rank = jnp.sum(present[..., :, None] * earlier.astype(jnp.int32), axis=-2)
    slot_hit = (
        (present[..., None] == 1) & (slot_rank[..., None] == jnp.arange(capacity))
    ).astype(jnp.int32)
    request = jnp.sum(slot_hit * jnp.arange(own_blocks)[:, None], axis=2)
    asked = lax.all_to_all(
        request.transpose(1, 0, 2), "ctx", split_axis=0, concat_axis=0, tiled=True
    )
    head_pick = jnp.arange(kv_heads)[None, :, None]
    send = pieces[head_pick, asked]
    got = lax.all_to_all(send, "ctx", split_axis=0, concat_axis=0, tiled=True)
    others = (my_index + 1 + jnp.arange(ctx_count - 1)) % ctx_count
    got = got[others]
    remote_slots = (ctx_count - 1) * capacity
    slots = remote_slots + own_blocks
    got = got.transpose(3, 1, 0, 2, 4, 5).reshape(2, kv_heads, remote_slots * span, head_dim)
    local = pieces.transpose(2, 0, 1, 3, 4).reshape(2, kv_heads, tokens_dev, head_dim)
    both = jnp.concatenate([got, local], axis=2)
    slot_on = jnp.einsum("jhob,hobc->jhoc", hits, slot_hit)[:, :, others].reshape(
        own_blocks, kv_heads, remote_slots
    )
    local_on = lax.dynamic_index_in_dim(hits, my_index, axis=2, keepdims=False)
    below = jnp.arange(own_blocks)[None, :] < jnp.arange(own_blocks)[:, None]
    local_on = local_on * below.astype(jnp.int32)[:, None, :]
    bias = jnp.where(jnp.concatenate([slot_on, local_on], axis=-1) > 0, 0.0, MASKED)
    bias = bias.astype(jnp.float32).reshape(-1)
    dims = (
        kv_heads,
        group,
        span,
        remote_slots,
        own_blocks,
        capacity,
        kv_heads if slots <= 40 else 1,
    )
    gate_pairs = gate_weights.reshape(kv_heads, group, 2, head_dim).transpose(0, 2, 1, 3)
    first = (my_index * own_blocks).astype(jnp.int32).reshape(1)
    key_acc, value_acc, comp_key_acc, comp_value_acc, gate_acc = attend(
        queries[0],
        teacher_out[0],
        both[0],
        both[1],
        comp_keys,
        comp_values,
        gate_pairs,
        bias,
        first,
        dims,
    )
    accs = jnp.stack([key_acc, value_acc]).reshape(2, kv_heads, slots, span, head_dim)
    back = accs[:, :, :remote_slots].reshape(
        2, kv_heads, ctx_count - 1, capacity, span, head_dim
    ).transpose(2, 1, 3, 0, 4, 5)
    back = jnp.concatenate([back, jnp.zeros_like(back[:1])], axis=0)
    back = back[(jnp.arange(ctx_count) - my_index - 1) % ctx_count].astype(jnp.bfloat16)
    returned = lax.all_to_all(back, "ctx", split_axis=0, concat_axis=0, tiled=True)
    place = (asked[..., None] == jnp.arange(own_blocks)).astype(jnp.bfloat16)
    added = jnp.einsum(
        "ohcb,ohcrud->rhbud", place, returned, preferred_element_type=jnp.float32
    )
    piece_grad = accs[:, :, remote_slots:] + added
    comp_own = lax.psum_scatter(
        jnp.stack([comp_key_acc, comp_value_acc]), "ctx", scatter_dimension=2, tiled=True
    )
    compress = jnp.stack([compress_keys, compress_values])
    totals = piece_grad + compress[:, :, None, :, :] * comp_own[:, :, :, None, :]
    grads = (
        totals.transpose(0, 2, 3, 1, 4)
        .reshape(2, tokens_dev, kv_heads, head_dim)
        .astype(jnp.bfloat16)
    )
    weight_grads = jnp.sum(
        comp_own[:, :, :, None, :] * local.reshape(piece_grad.shape).astype(jnp.float32), axis=2
    )
    gate_part = gate_acc.transpose(0, 2, 1, 3).reshape(kv_heads * group, 2, head_dim)
    summed = lax.psum((weight_grads, gate_part), ("ctx", "dp"))
    divisor = math.sqrt(lax.axis_size("dp") * ctx_count * tokens_dev)
    return (
        grads[0][None],
        grads[1][None],
        summed[0][0] / divisor,
        summed[0][1] / divisor,
        summed[1] / divisor,
    )


def solution(mesh):
    tokens = P(("groups", "dp"), "ctx", "head", None)
    weights = P("head", None, None)
    sums = P(("groups", "head"), None, None)
    return jax.shard_map(
        on_device,
        mesh=mesh,
        in_specs=(tokens,) * 5 + (weights,) * 3,
        out_specs=(tokens, tokens, sums, sums, sums),
        check_vma=False,
    )
```

```python
import functools
import math

import jax
import jax.numpy as jnp
from jax import lax
from jax.experimental import pallas as pl
from jax.experimental.pallas import tpu as pltpu
from jax.sharding import PartitionSpec as P

HIGHEST = lax.Precision.HIGHEST
MASKED = -1e30
NT = (((1,), (1,)), ((), ()))
NN = (((1,), (0,)), ((), ()))
TN = (((0,), (0,)), ((), ()))


def dot(a, b, dims):
    return lax.dot_general(a, b, dims, preferred_element_type=jnp.float32)


def fold(x, op):
    return op(x.reshape(x.shape[0] // 8, 8, x.shape[1]), axis=0)


def attend_kernel(
    dims,
    bias_ref,
    q_ref,
    t_ref,
    k_ref,
    v_ref,
    ck_ref,
    cv_ref,
    gw_ref,
    cur_ref,
    dk_ref,
    dv_ref,
    dck_ref,
    dcv_ref,
    dgw_ref,
    s_scr,
    d_scr,
    vt_scr,
    ot_scr,
    tri_scr,
):
    kv_heads, group, span, remote_slots, own_blocks, chunk_slots, pair = dims
    slots = remote_slots + own_blocks
    chunk = chunk_slots * span
    head_dim = q_ref.shape[-1]
    rows = span * group
    factor = head_dim ** (-0.5)
    power = factor * math.log2(math.e)
    j = pl.program_id(0)
    chunks = (remote_slots + j) // chunk_slots + 1

    @pl.when(j == 0)
    def _():
        dk_ref[...] = jnp.zeros_like(dk_ref)
        dv_ref[...] = jnp.zeros_like(dv_ref)
        dck_ref[...] = jnp.zeros_like(dck_ref)
        dcv_ref[...] = jnp.zeros_like(dcv_ref)
        dgw_ref[...] = jnp.zeros_like(dgw_ref)
        key_at = lax.broadcasted_iota(jnp.int32, (span, rows), 0)
        row_at = lax.broadcasted_iota(jnp.int32, (span, rows), 1) // group
        tri_scr[...] = jnp.where(key_at <= row_at, 0.0, MASKED)

        def turn(c, _):
            at = pl.ds(pl.multiple_of(c * chunk, chunk), chunk)
            for g in range(kv_heads):
                vt_scr[g, :, at] = v_ref[g, at, :].astype(jnp.float32).T.astype(jnp.bfloat16)
            return 0

        lax.fori_loop(0, slots // chunk_slots, turn, 0)

    for base in range(0, kv_heads, pair):
        heads = [(p, base + p) for p in range(pair)]
        wide = {}
        narrow = {}
        for p, g in heads:
            wide[p] = (
                q_ref[...].astype(jnp.float32)[:, g * group : (g + 1) * group, :]
            )
            narrow[p] = wide[p].reshape(rows, head_dim).astype(jnp.bfloat16)

        def scores(c, peaks):
            at = pl.ds(pl.multiple_of(c * chunk, chunk), chunk)
            out = []
            for p, g in heads:
                s = dot(k_ref[g, at, :], narrow[p], NT)
                parts = []
                for i in range(chunk_slots):
                    b = bias_ref[(j * kv_heads + g) * slots + c * chunk_slots + i]
                    parts.append(s[i * span : (i + 1) * span] + b)
                s = jnp.concatenate(parts, axis=0)
                s_scr[p, at, :] = s
                out.append(jnp.maximum(peaks[p], fold(s, jnp.max)))
            return tuple(out)

        peaks = lax.fori_loop(
            0, chunks, scores, tuple(jnp.full((8, rows), MASKED, jnp.float32) for _ in heads)
        )
        own = pl.ds(pl.multiple_of((remote_slots + j) * span, span), span)
        peak = {}
        for p, g in heads:
            s = dot(k_ref[g, own, :], narrow[p], NT) + tri_scr[...]
            s_scr[p, own, :] = s
            peak[p] = jnp.max(
                jnp.maximum(peaks[p], fold(s, jnp.max)), axis=0, keepdims=True
            )

        def raise_all(c, sums):
            at = pl.ds(pl.multiple_of(c * chunk, chunk), chunk)
            out = []
            for p, g in heads:
                e = jnp.exp2((s_scr[p, at, :] - peak[p]) * power)
                s_scr[p, at, :] = e
                out.append(sums[p] + fold(e, jnp.sum))
            return tuple(out)

        sums = lax.fori_loop(
            0, chunks, raise_all, tuple(jnp.zeros((8, rows), jnp.float32) for _ in heads)
        )
        inverse = {p: 1.0 / jnp.sum(sums[p], axis=0, keepdims=True) for p, g in heads}
        ot_scr[...] = jnp.zeros_like(ot_scr)

        def outputs(c, _):
            at = pl.ds(pl.multiple_of(c * chunk, chunk), chunk)
            for p, g in heads:
                w = s_scr[p, at, :] * inverse[p]
                s_scr[p, at, :] = w
                ot_scr[p] += dot(vt_scr[g, :, at], w.astype(jnp.bfloat16), NN)
            return 0

        lax.fori_loop(0, chunks, outputs, 0)

        backs = {}
        for p, g in heads:
            sel_out = ot_scr[p].T
            ck = ck_ref[g]
            cv = cv_ref[g]
            cs = dot(ck, narrow[p], NT)
            at_block = lax.broadcasted_iota(jnp.int32, cs.shape, 0)
            usable = at_block <= cur_ref[0] + j
            cs = jnp.where(usable, cs, MASKED)
            ce = jnp.exp2((cs - jnp.max(cs, axis=0, keepdims=True)) * power)
            cw = ce * (1.0 / jnp.sum(ce, axis=0, keepdims=True))
            cr = cw.astype(jnp.bfloat16)
            comp_out = dot(cv, cr, TN).T
            q3 = wide[p]
            gates = []
            for r in range(2):
                logit = jnp.sum(q3 * gw_ref[g, r][None], axis=-1, keepdims=True)
                gates.append(jax.nn.sigmoid(logit))
            comp3 = comp_out.reshape(span, group, head_dim)
            sel3 = sel_out.reshape(span, group, head_dim)
            t3 = t_ref[...].astype(jnp.float32)[:, g * group : (g + 1) * group, :]
            error = gates[0] * comp3 + gates[1] * sel3 - t3
            for r, branch in ((0, comp3), (1, sel3)):
                term = jnp.sum(error * branch, axis=-1, keepdims=True) * (
                    gates[r] * (1.0 - gates[r])
                )
                dgw_ref[g, r] += jnp.sum(term * q3, axis=0)
            backs[p] = (gates[1] * error).reshape(rows, head_dim).astype(jnp.bfloat16)
            cb = (gates[0] * error).reshape(rows, head_dim).astype(jnp.bfloat16)
            cd = dot(cv, cb, NT)
            total = jnp.sum(cw * cd, axis=0, keepdims=True)
            cg = (factor * cw * (cd - total)).astype(jnp.bfloat16)
            dck_ref[g] += dot(cg, narrow[p], NN)
            dcv_ref[g] += dot(cr, cb, NN)

        def weight_grads(c, totals):
            at = pl.ds(pl.multiple_of(c * chunk, chunk), chunk)
            out = []
            for p, g in heads:
                d = dot(v_ref[g, at, :], backs[p], NT)
                d_scr[p, at, :] = d
                out.append(totals[p] + fold(s_scr[p, at, :] * d, jnp.sum))
            return tuple(out)

        totals = lax.fori_loop(
            0, chunks, weight_grads, tuple(jnp.zeros((8, rows), jnp.float32) for _ in heads)
        )
        total = {p: jnp.sum(totals[p], axis=0, keepdims=True) for p, g in heads}

        def key_grads(c, _):
            at = pl.ds(pl.multiple_of(c * chunk, chunk), chunk)
            for p, g in heads:
                w = s_scr[p, at, :]
                sg = (w * ((d_scr[p, at, :] - total[p]) * factor)).astype(jnp.bfloat16)
                dk_ref[g, at, :] += dot(sg, narrow[p], NN)
                dv_ref[g, at, :] += dot(w.astype(jnp.bfloat16), backs[p], NN)
            return 0

        lax.fori_loop(0, chunks, key_grads, 0)


def attend(queries, teacher, keys, values, comp_keys, comp_values, gate_pairs, bias, first, dims):
    kv_heads, group, span, remote_slots, own_blocks, chunk_slots, pair = dims
    slots = remote_slots + own_blocks
    head_dim = keys.shape[-1]
    all_blocks = comp_keys.shape[1]
    rows = span * group
    whole = pl.BlockSpec(memory_space=pltpu.VMEM)
    scalars = pl.BlockSpec(memory_space=pltpu.SMEM)
    tokens = pl.BlockSpec((span, kv_heads * group, head_dim), lambda j: (j, 0, 0))
    f32 = jnp.float32
    flops = own_blocks * kv_heads * rows * slots * span * head_dim * 10
    return pl.pallas_call(
        functools.partial(attend_kernel, dims),
        grid=(own_blocks,),
        in_specs=[scalars, tokens, tokens, whole, whole, whole, whole, whole, scalars],
        out_specs=[whole] * 5,
        out_shape=[
            jax.ShapeDtypeStruct((kv_heads, slots * span, head_dim), f32),
            jax.ShapeDtypeStruct((kv_heads, slots * span, head_dim), f32),
            jax.ShapeDtypeStruct((kv_heads, all_blocks, head_dim), f32),
            jax.ShapeDtypeStruct((kv_heads, all_blocks, head_dim), f32),
            jax.ShapeDtypeStruct((kv_heads, 2, group, head_dim), f32),
        ],
        scratch_shapes=[
            pltpu.VMEM((pair, slots * span, rows), f32),
            pltpu.VMEM((pair, slots * span, rows), f32),
            pltpu.VMEM((kv_heads, head_dim, slots * span), jnp.bfloat16),
            pltpu.VMEM((pair, head_dim, rows), f32),
            pltpu.VMEM((span, rows), f32),
        ],
        compiler_params=pltpu.CompilerParams(vmem_limit_bytes=60 * 1024 * 1024),
        cost_estimate=pl.CostEstimate(flops=flops, bytes_accessed=8 << 20, transcendentals=0),
    )(bias, queries, teacher, keys, values, comp_keys, comp_values, gate_pairs, first)


def sum_everywhere(rows, axes):
    count = math.prod(lax.axis_size(axis) for axis in axes)
    total, lanes = rows.shape
    share = -(-total // (8 * count)) * 8
    padded = jnp.pad(rows, ((0, share * count - total), (0, 0))).reshape(count, share, lanes)
    parts = lax.all_to_all(padded, axes, split_axis=0, concat_axis=0, tiled=True)
    mine = jnp.broadcast_to(jnp.sum(parts, axis=0)[None], parts.shape)
    every = lax.all_to_all(mine, axes, split_axis=0, concat_axis=0, tiled=True)
    return every.reshape(share * count, lanes)[:total]


def on_device(
    queries,
    key_states,
    value_states,
    teacher_out,
    selection,
    compress_keys,
    compress_values,
    gate_weights,
):
    ctx_count = lax.axis_size("ctx")
    my_index = lax.axis_index("ctx")
    tokens_dev = key_states.shape[1]
    kv_heads = key_states.shape[2]
    head_dim = key_states.shape[3]
    span = compress_keys.shape[1]
    own_blocks = tokens_dev // span
    all_blocks = own_blocks * ctx_count
    group = queries.shape[2] // kv_heads
    key_blocks = key_states[0].reshape(own_blocks, span, kv_heads, head_dim)
    value_blocks = value_states[0].reshape(own_blocks, span, kv_heads, head_dim)
    comp_local = jnp.stack(
        [
            jnp.sum(key_blocks.astype(jnp.float32) * compress_keys.transpose(1, 0, 2)[None], axis=1),
            jnp.sum(
                value_blocks.astype(jnp.float32) * compress_values.transpose(1, 0, 2)[None], axis=1
            ),
        ]
    ).astype(jnp.bfloat16)
    chosen = selection[0]
    pieces = jnp.stack(
        [key_blocks.transpose(2, 0, 1, 3), value_blocks.transpose(2, 0, 1, 3)], axis=2
    )
    capacity = own_blocks // 2
    hits = jnp.any(chosen[..., None] == jnp.arange(all_blocks), axis=2)
    hits = hits.astype(jnp.int32).reshape(own_blocks, kv_heads, ctx_count, own_blocks)
    present = jnp.max(hits, axis=0)
    earlier = jnp.arange(own_blocks)[:, None] < jnp.arange(own_blocks)[None, :]
    slot_rank = jnp.sum(present[..., :, None] * earlier.astype(jnp.int32), axis=-2)
    slot_hit = (
        (present[..., None] == 1) & (slot_rank[..., None] == jnp.arange(capacity))
    ).astype(jnp.int32)
    request = jnp.sum(slot_hit * jnp.arange(own_blocks)[:, None], axis=2)
    asked = lax.all_to_all(
        request.transpose(1, 0, 2), "ctx", split_axis=0, concat_axis=0, tiled=True
    )
    head_pick = jnp.arange(kv_heads)[None, :, None]
    send = pieces[head_pick, asked].reshape(ctx_count, -1, head_dim)
    comp_rows = comp_local.transpose(0, 2, 1, 3).reshape(-1, head_dim)
    comp_send = jnp.broadcast_to(comp_rows[None], (ctx_count,) + comp_rows.shape)
    mixed = lax.all_to_all(
        jnp.concatenate([send, comp_send], axis=1), "ctx", split_axis=0, concat_axis=0, tiled=True
    )
    got = mixed[:, : send.shape[1]].reshape(ctx_count, kv_heads, capacity, 2, span, head_dim)
    comp_all = mixed[:, send.shape[1] :].reshape(ctx_count, 2, kv_heads, own_blocks, head_dim)
    comp_all = comp_all.transpose(1, 2, 0, 3, 4).reshape(2, kv_heads, all_blocks, head_dim)
    comp_keys, comp_values = comp_all[0], comp_all[1]
    others = (my_index + 1 + jnp.arange(ctx_count - 1)) % ctx_count
    got = got[others]
    remote_slots = (ctx_count - 1) * capacity
    slots = remote_slots + own_blocks
    got = got.transpose(3, 1, 0, 2, 4, 5).reshape(2, kv_heads, remote_slots * span, head_dim)
    local = pieces.transpose(2, 0, 1, 3, 4).reshape(2, kv_heads, tokens_dev, head_dim)
    both = jnp.concatenate([got, local], axis=2)
    slot_on = jnp.einsum("jhob,hobc->jhoc", hits, slot_hit)[:, :, others].reshape(
        own_blocks, kv_heads, remote_slots
    )
    local_on = lax.dynamic_index_in_dim(hits, my_index, axis=2, keepdims=False)
    below = jnp.arange(own_blocks)[None, :] < jnp.arange(own_blocks)[:, None]
    local_on = local_on * below.astype(jnp.int32)[:, None, :]
    bias = jnp.where(jnp.concatenate([slot_on, local_on], axis=-1) > 0, 0.0, MASKED)
    bias = bias.astype(jnp.float32).reshape(-1)
    dims = (
        kv_heads,
        group,
        span,
        remote_slots,
        own_blocks,
        capacity,
        kv_heads if slots <= 40 else 1,
    )
    gate_pairs = gate_weights.reshape(kv_heads, group, 2, head_dim).transpose(0, 2, 1, 3)
    first = (my_index * own_blocks).astype(jnp.int32).reshape(1)
    key_acc, value_acc, comp_key_acc, comp_value_acc, gate_acc = attend(
        queries[0],
        teacher_out[0],
        both[0],
        both[1],
        comp_keys,
        comp_values,
        gate_pairs,
        bias,
        first,
        dims,
    )
    accs = jnp.stack([key_acc, value_acc]).reshape(2, kv_heads, slots, span, head_dim)
    back = accs[:, :, :remote_slots].reshape(
        2, kv_heads, ctx_count - 1, capacity, span, head_dim
    ).transpose(2, 1, 3, 0, 4, 5)
    back = jnp.concatenate([back, jnp.zeros_like(back[:1])], axis=0)
    back = back[(jnp.arange(ctx_count) - my_index - 1) % ctx_count].astype(jnp.bfloat16)
    returned = lax.all_to_all(back, "ctx", split_axis=0, concat_axis=0, tiled=True)
    place = (asked[..., None] == jnp.arange(own_blocks)).astype(jnp.bfloat16)
    added = jnp.einsum(
        "ohcb,ohcrud->rhbud", place, returned, preferred_element_type=jnp.float32
    )
    piece_grad = accs[:, :, remote_slots:] + added
    comp_parts = jnp.stack([comp_key_acc, comp_value_acc]).reshape(
        2, kv_heads, ctx_count, own_blocks, head_dim
    )
    comp_own = jnp.sum(
        lax.all_to_all(
            comp_parts.transpose(2, 0, 1, 3, 4), "ctx", split_axis=0, concat_axis=0, tiled=True
        ),
        axis=0,
    )
    compress = jnp.stack([compress_keys, compress_values])
    totals = piece_grad + compress[:, :, None, :, :] * comp_own[:, :, :, None, :]
    grads = (
        totals.transpose(0, 2, 3, 1, 4)
        .reshape(2, tokens_dev, kv_heads, head_dim)
        .astype(jnp.bfloat16)
    )
    weight_grads = jnp.sum(
        comp_own[:, :, :, None, :] * local.reshape(piece_grad.shape).astype(jnp.float32), axis=2
    )
    gate_part = gate_acc.transpose(0, 2, 1, 3).reshape(kv_heads * group, 2, head_dim)
    flat = jnp.concatenate(
        [weight_grads.reshape(-1, head_dim), gate_part.reshape(-1, head_dim)], axis=0
    )
    flat = sum_everywhere(flat, ("ctx", "dp"))
    weight_rows = 2 * kv_heads * span
    summed = (
        flat[:weight_rows].reshape(weight_grads.shape),
        flat[weight_rows:].reshape(gate_part.shape),
    )
    divisor = math.sqrt(lax.axis_size("dp") * ctx_count * tokens_dev)
    return (
        grads[0][None],
        grads[1][None],
        summed[0][0] / divisor,
        summed[0][1] / divisor,
        summed[1] / divisor,
    )


def solution(mesh):
    tokens = P(("groups", "dp"), "ctx", "head", None)
    weights = P("head", None, None)
    sums = P(("groups", "head"), None, None)
    return jax.shard_map(
        on_device,
        mesh=mesh,
        in_specs=(tokens,) * 5 + (weights,) * 3,
        out_specs=(tokens, tokens, sums, sums, sums),
        check_vma=False,
    )
```

```python
import functools
import math

import jax
import jax.numpy as jnp
from jax import lax
from jax.experimental import pallas as pl
from jax.experimental.pallas import tpu as pltpu
from jax.sharding import PartitionSpec as P

HIGHEST = lax.Precision.HIGHEST
MASKED = -1e30
NT = (((1,), (1,)), ((), ()))
NN = (((1,), (0,)), ((), ()))
TN = (((0,), (0,)), ((), ()))


def dot(a, b, dims):
    return lax.dot_general(a, b, dims, preferred_element_type=jnp.float32)


UNROLL = 20


def span_of(c, size):
    return pl.ds(c * size if isinstance(c, int) else pl.multiple_of(c * size, size), size)


def sweep(slots, chunk_slots, used, body, start):
    if slots <= UNROLL:
        for c in range(slots // chunk_slots):
            start = body(c, start)
        return start
    return lax.fori_loop(0, used, body, start)


def fold(x, op):
    return op(x.reshape(x.shape[0] // 8, 8, x.shape[1]), axis=0)


def attend_kernel(
    dims,
    bias_ref,
    q_ref,
    t_ref,
    k_ref,
    v_ref,
    ck_ref,
    cv_ref,
    gw_ref,
    cur_ref,
    dk_ref,
    dv_ref,
    dck_ref,
    dcv_ref,
    dgw_ref,
    s_scr,
    d_scr,
    vt_scr,
    ot_scr,
    tri_scr,
):
    kv_heads, group, span, remote_slots, own_blocks, chunk_slots, pair, offset = dims
    slots = remote_slots + own_blocks
    chunk = chunk_slots * span
    head_dim = q_ref.shape[-1]
    rows = span * group
    factor = head_dim ** (-0.5)
    power = factor * math.log2(math.e)
    j = pl.program_id(0)
    chunks = (remote_slots + j) // chunk_slots + 1

    @pl.when(j == 0)
    def _():
        dk_ref[...] = jnp.zeros_like(dk_ref)
        dv_ref[...] = jnp.zeros_like(dv_ref)
        dck_ref[...] = jnp.zeros_like(dck_ref)
        dcv_ref[...] = jnp.zeros_like(dcv_ref)
        dgw_ref[...] = jnp.zeros_like(dgw_ref)
        key_at = lax.broadcasted_iota(jnp.int32, (span, rows), 0)
        row_at = lax.broadcasted_iota(jnp.int32, (span, rows), 1) // group
        tri_scr[...] = jnp.where(key_at <= row_at, 0.0, MASKED)

        def turn(c, _):
            at = span_of(c, chunk)
            for g in range(kv_heads):
                vt_scr[g, :, at] = v_ref[g, at, :].astype(jnp.float32).T.astype(jnp.bfloat16)
            return 0

        lax.fori_loop(0, slots // chunk_slots, turn, 0)

    for base in range(0, kv_heads, pair):
        heads = [(p, base + p) for p in range(pair)]
        wide = {}
        narrow = {}
        for p, g in heads:
            wide[p] = (
                q_ref[...].astype(jnp.float32)[:, (offset + g) * group : (offset + g + 1) * group, :]
            )
            narrow[p] = wide[p].reshape(rows, head_dim).astype(jnp.bfloat16)

        def scores(c, peaks):
            at = span_of(c, chunk)
            out = []
            for p, g in heads:
                s = dot(k_ref[g, at, :], narrow[p], NT)
                parts = []
                for i in range(chunk_slots):
                    b = bias_ref[(j * kv_heads + g) * slots + c * chunk_slots + i]
                    parts.append(s[i * span : (i + 1) * span] + b)
                s = jnp.concatenate(parts, axis=0)
                s_scr[p, at, :] = s
                out.append(jnp.maximum(peaks[p], fold(s, jnp.max)))
            return tuple(out)

        peaks = sweep(
            slots, chunk_slots, chunks, scores, tuple(jnp.full((8, rows), MASKED, jnp.float32) for _ in heads)
        )
        own = pl.ds(pl.multiple_of((remote_slots + j) * span, span), span)
        peak = {}
        for p, g in heads:
            s = dot(k_ref[g, own, :], narrow[p], NT) + tri_scr[...]
            s_scr[p, own, :] = s
            peak[p] = jnp.max(
                jnp.maximum(peaks[p], fold(s, jnp.max)), axis=0, keepdims=True
            )

        def raise_all(c, sums):
            at = span_of(c, chunk)
            out = []
            for p, g in heads:
                e = jnp.exp2((s_scr[p, at, :] - peak[p]) * power)
                s_scr[p, at, :] = e
                out.append(sums[p] + fold(e, jnp.sum))
            return tuple(out)

        sums = sweep(
            slots, chunk_slots, chunks, raise_all, tuple(jnp.zeros((8, rows), jnp.float32) for _ in heads)
        )
        inverse = {p: 1.0 / jnp.sum(sums[p], axis=0, keepdims=True) for p, g in heads}
        ot_scr[...] = jnp.zeros_like(ot_scr)

        def outputs(c, _):
            at = span_of(c, chunk)
            for p, g in heads:
                w = s_scr[p, at, :] * inverse[p]
                s_scr[p, at, :] = w
                ot_scr[p] += dot(vt_scr[g, :, at], w.astype(jnp.bfloat16), NN)
            return 0

        sweep(slots, chunk_slots, chunks, outputs, 0)

        backs = {}
        for p, g in heads:
            sel_out = ot_scr[p].T
            ck = ck_ref[g]
            cv = cv_ref[g]
            cs = dot(ck, narrow[p], NT)
            all_blocks = cs.shape[0]
            at_block = lax.broadcasted_iota(jnp.int32, cs.shape, 0)
            usable = (at_block + cur_ref[0] >= 0) & (at_block <= all_blocks - own_blocks + j)
            cs = jnp.where(usable, cs, MASKED)
            ce = jnp.exp2((cs - jnp.max(cs, axis=0, keepdims=True)) * power)
            cw = ce * (1.0 / jnp.sum(ce, axis=0, keepdims=True))
            cr = cw.astype(jnp.bfloat16)
            comp_out = dot(cv, cr, TN).T
            q3 = wide[p]
            gates = []
            for r in range(2):
                logit = jnp.sum(q3 * gw_ref[g, r][None], axis=-1, keepdims=True)
                gates.append(jax.nn.sigmoid(logit))
            comp3 = comp_out.reshape(span, group, head_dim)
            sel3 = sel_out.reshape(span, group, head_dim)
            t3 = t_ref[...].astype(jnp.float32)[
                :, (offset + g) * group : (offset + g + 1) * group, :
            ]
            error = gates[0] * comp3 + gates[1] * sel3 - t3
            for r, branch in ((0, comp3), (1, sel3)):
                term = jnp.sum(error * branch, axis=-1, keepdims=True) * (
                    gates[r] * (1.0 - gates[r])
                )
                dgw_ref[g, r] += jnp.sum(term * q3, axis=0)
            backs[p] = (gates[1] * error).reshape(rows, head_dim).astype(jnp.bfloat16)
            cb = (gates[0] * error).reshape(rows, head_dim).astype(jnp.bfloat16)
            cd = dot(cv, cb, NT)
            total = jnp.sum(cw * cd, axis=0, keepdims=True)
            cg = (factor * cw * (cd - total)).astype(jnp.bfloat16)
            dck_ref[g] += dot(cg, narrow[p], NN)
            dcv_ref[g] += dot(cr, cb, NN)

        def weight_grads(c, totals):
            at = span_of(c, chunk)
            out = []
            for p, g in heads:
                d = dot(v_ref[g, at, :], backs[p], NT)
                d_scr[p, at, :] = d
                out.append(totals[p] + fold(s_scr[p, at, :] * d, jnp.sum))
            return tuple(out)

        totals = sweep(
            slots, chunk_slots, chunks, weight_grads, tuple(jnp.zeros((8, rows), jnp.float32) for _ in heads)
        )
        total = {p: jnp.sum(totals[p], axis=0, keepdims=True) for p, g in heads}

        def key_grads(c, _):
            at = span_of(c, chunk)
            for p, g in heads:
                w = s_scr[p, at, :]
                sg = (w * ((d_scr[p, at, :] - total[p]) * factor)).astype(jnp.bfloat16)
                dk_ref[g, at, :] += dot(sg, narrow[p], NN)
                dv_ref[g, at, :] += dot(w.astype(jnp.bfloat16), backs[p], NN)
            return 0

        sweep(slots, chunk_slots, chunks, key_grads, 0)


def attend(queries, teacher, keys, values, comp_keys, comp_values, gate_pairs, bias, first, dims):
    kv_heads, group, span, remote_slots, own_blocks, chunk_slots, pair, offset = dims
    slots = remote_slots + own_blocks
    head_dim = keys.shape[-1]
    all_blocks = comp_keys.shape[1]
    rows = span * group
    whole = pl.BlockSpec(memory_space=pltpu.VMEM)
    scalars = pl.BlockSpec(memory_space=pltpu.SMEM)
    tokens = pl.BlockSpec((span, queries.shape[1], head_dim), lambda j: (j, 0, 0))
    f32 = jnp.float32
    flops = own_blocks * kv_heads * rows * slots * span * head_dim * 10
    return pl.pallas_call(
        functools.partial(attend_kernel, dims),
        grid=(own_blocks,),
        in_specs=[scalars, tokens, tokens, whole, whole, whole, whole, whole, scalars],
        out_specs=[whole] * 5,
        out_shape=[
            jax.ShapeDtypeStruct((kv_heads, slots * span, head_dim), f32),
            jax.ShapeDtypeStruct((kv_heads, slots * span, head_dim), f32),
            jax.ShapeDtypeStruct((kv_heads, all_blocks, head_dim), f32),
            jax.ShapeDtypeStruct((kv_heads, all_blocks, head_dim), f32),
            jax.ShapeDtypeStruct((kv_heads, 2, group, head_dim), f32),
        ],
        scratch_shapes=[
            pltpu.VMEM((pair, slots * span, rows), f32),
            pltpu.VMEM((pair, slots * span, rows), f32),
            pltpu.VMEM((kv_heads, head_dim, slots * span), jnp.bfloat16),
            pltpu.VMEM((pair, head_dim, rows), f32),
            pltpu.VMEM((span, rows), f32),
        ],
        compiler_params=pltpu.CompilerParams(vmem_limit_bytes=60 * 1024 * 1024),
        cost_estimate=pl.CostEstimate(flops=flops, bytes_accessed=8 << 20, transcendentals=0),
    )(bias, queries, teacher, keys, values, comp_keys, comp_values, gate_pairs, first)


def sum_everywhere(rows, axes):
    count = math.prod(lax.axis_size(axis) for axis in axes)
    total, lanes = rows.shape
    share = -(-total // (8 * count)) * 8
    padded = jnp.pad(rows, ((0, share * count - total), (0, 0))).reshape(count, share, lanes)
    parts = lax.all_to_all(padded, axes, split_axis=0, concat_axis=0, tiled=True)
    mine = jnp.broadcast_to(jnp.sum(parts, axis=0)[None], parts.shape)
    every = lax.all_to_all(mine, axes, split_axis=0, concat_axis=0, tiled=True)
    return every.reshape(share * count, lanes)[:total]


def on_device(
    queries,
    key_states,
    value_states,
    teacher_out,
    selection,
    compress_keys,
    compress_values,
    gate_weights,
):
    ctx_count = lax.axis_size("ctx")
    my_index = lax.axis_index("ctx")
    tokens_dev = key_states.shape[1]
    kv_heads = key_states.shape[2]
    head_dim = key_states.shape[3]
    span = compress_keys.shape[1]
    own_blocks = tokens_dev // span
    all_blocks = own_blocks * ctx_count
    group = queries.shape[2] // kv_heads
    both = jnp.stack([key_states[0], value_states[0]]).reshape(
        2, own_blocks, span, kv_heads, head_dim
    )
    compress = jnp.stack([compress_keys, compress_values])
    comp_local = jnp.sum(
        both.astype(jnp.float32) * compress.transpose(0, 2, 1, 3)[:, None], axis=2
    ).astype(jnp.bfloat16)
    local = both.transpose(3, 0, 1, 2, 4)
    chosen = selection[0]
    capacity = own_blocks // 2
    hits = jnp.any(chosen[..., None] == jnp.arange(all_blocks), axis=2)
    hits = hits.astype(jnp.int32).reshape(own_blocks, kv_heads, ctx_count, own_blocks)
    present = jnp.max(hits, axis=0)
    earlier = jnp.arange(own_blocks)[:, None] < jnp.arange(own_blocks)[None, :]
    slot_rank = jnp.sum(present[..., :, None] * earlier.astype(jnp.int32), axis=-2)
    slot_hit = (
        (present[..., None] == 1) & (slot_rank[..., None] == jnp.arange(capacity))
    ).astype(jnp.int32)
    request = jnp.sum(slot_hit * jnp.arange(own_blocks)[:, None], axis=2)
    asked = lax.all_to_all(
        request.transpose(1, 0, 2), "ctx", split_axis=0, concat_axis=0, tiled=True
    )
    shifts = range(1, ctx_count)
    above = asked[(my_index + jnp.arange(1, ctx_count)) % ctx_count]
    others = (my_index - jnp.arange(1, ctx_count)) % ctx_count
    remote_slots = (ctx_count - 1) * capacity
    slots = remote_slots + own_blocks
    slot_on = jnp.einsum("jhob,hobc->jhoc", hits, slot_hit)[:, :, others].reshape(
        own_blocks, kv_heads, remote_slots
    )
    local_on = lax.dynamic_index_in_dim(hits, my_index, axis=2, keepdims=False)
    below = jnp.arange(own_blocks)[None, :] < jnp.arange(own_blocks)[:, None]
    local_on = local_on * below.astype(jnp.int32)[:, None, :]
    bias = jnp.where(jnp.concatenate([slot_on, local_on], axis=-1) > 0, 0.0, MASKED)
    bias = bias.astype(jnp.float32)
    gate_pairs = gate_weights.reshape(kv_heads, group, 2, head_dim).transpose(0, 2, 1, 3)
    first = ((my_index - ctx_count + 1) * own_blocks).astype(jnp.int32).reshape(1)
    piece_rows = capacity * span

    def up(x, shift):
        return lax.ppermute(x, "ctx", [(i, i + shift) for i in range(ctx_count - shift)])

    def down(x, shift):
        return lax.ppermute(x, "ctx", [(i + shift, i) for i in range(ctx_count - shift)])

    arrived = []
    for h in range(kv_heads):
        parts = []
        for shift in shifts:
            picked = local[h][:, above[shift - 1, h]].reshape(2, piece_rows, head_dim)
            parts.append(up(jnp.concatenate([picked, comp_local[:, :, h]], axis=1), shift))
        arrived.append(parts)
    key_value_back = []
    comp_sums = []
    gate_sums = []
    for h in range(kv_heads):
        parts = arrived[h]
        pieces = jnp.concatenate(
            [part[:, :piece_rows] for part in parts] + [local[h].reshape(2, -1, head_dim)], axis=1
        )
        comp = jnp.concatenate(
            [part[:, piece_rows:] for part in parts[::-1]] + [comp_local[:, :, h]], axis=1
        )
        dims = (
            1,
            group,
            span,
            remote_slots,
            own_blocks,
            slots if slots <= UNROLL else capacity,
            1,
            h,
        )
        key_acc, value_acc, comp_key, comp_value, gate_acc = attend(
            queries[0],
            teacher_out[0],
            pieces[0][None],
            pieces[1][None],
            comp[0][None],
            comp[1][None],
            gate_pairs[h][None],
            bias[:, h].reshape(-1),
            first,
            dims,
        )
        if key_value_back:
            own, returned = key_value_back[-1]
            key_acc, value_acc, comp_key, comp_value, gate_acc, returned = lax.optimization_barrier(
                (key_acc, value_acc, comp_key, comp_value, gate_acc, returned)
            )
            key_value_back[-1] = (own, returned)
        accs = jnp.concatenate([key_acc, value_acc])
        returned = [
            down(
                accs[:, (shift - 1) * piece_rows : shift * piece_rows].astype(jnp.bfloat16), shift
            )
            for shift in shifts
        ]
        key_value_back.append((accs[:, remote_slots * span :], returned))
        comp_sums.append(jnp.concatenate([comp_key, comp_value]))
        gate_sums.append(gate_acc[0])
    comp_acc = jnp.stack(comp_sums).reshape(kv_heads, 2, ctx_count, own_blocks, head_dim)
    comp_own = comp_acc[:, :, ctx_count - 1]
    for shift in shifts:
        comp_own = comp_own + down(comp_acc[:, :, ctx_count - 1 - shift], shift)
    weight_grads = jnp.sum(comp_own[:, :, :, None, :] * local.astype(jnp.float32), axis=2)
    weight_grads = weight_grads.transpose(1, 0, 2, 3)
    gate_part = jnp.stack(gate_sums).transpose(0, 2, 1, 3).reshape(kv_heads * group, 2, head_dim)
    flat = jnp.concatenate(
        [weight_grads.reshape(-1, head_dim), gate_part.reshape(-1, head_dim)], axis=0
    )
    flat = sum_everywhere(flat, ("ctx", "dp"))
    weight_rows = 2 * kv_heads * span
    summed = (
        flat[:weight_rows].reshape(weight_grads.shape),
        flat[weight_rows:].reshape(gate_part.shape),
    )
    totals = []
    for h in range(kv_heads):
        own, returned = key_value_back[h]
        place = (above[:, h, :, None] == jnp.arange(own_blocks)).astype(jnp.bfloat16)
        place = place.transpose(2, 0, 1).reshape(own_blocks, remote_slots)
        stacked = jnp.stack(returned, axis=1).reshape(2, remote_slots, span, head_dim)
        added = jnp.einsum("bs,tsud->tbud", place, stacked, preferred_element_type=jnp.float32)
        total = own.reshape(added.shape) + added
        totals.append(total + compress[:, h][:, None] * comp_own[h][:, :, None, :])
    grads = jnp.stack(totals, axis=3).astype(jnp.bfloat16)
    grads = grads.reshape(2, tokens_dev, kv_heads, head_dim)
    divisor = math.sqrt(lax.axis_size("dp") * ctx_count * tokens_dev)
    return (
        grads[0][None],
        grads[1][None],
        summed[0][0] / divisor,
        summed[0][1] / divisor,
        summed[1] / divisor,
    )


def solution(mesh):
    tokens = P(("groups", "dp"), "ctx", "head", None)
    weights = P("head", None, None)
    sums = P(("groups", "head"), None, None)
    return jax.shard_map(
        on_device,
        mesh=mesh,
        in_specs=(tokens,) * 5 + (weights,) * 3,
        out_specs=(tokens, tokens, sums, sums, sums),
        check_vma=False,
    )
```
